32 devices in a mesh: expert: 4 (over y, x), tensor: 4 (over z), dp: 2 (over core).
Axes of the slice: x: 2, y: 2, z: 4, core: 2. Of those that a mesh axis runs over, the one named last changes fastest.
Arguments:
- out_grad: bfloat16 [4096, 2048], P(('expert', 'dp'), 'tensor'), may hold values from -1.5 to 1.5
- expert_ids: int32 [4096, 2], P(('expert', 'dp')), may hold values from 0 to 31, all different within a row; in each aligned block of 512 rows (0 to 511, 512 to 1023, ...) at most 36 rows name the same one
- gate_weights: float32 [4096, 2], P(('expert', 'dp')), may hold values from 0.05 to 1
- keep: int32 [4096, 2], P(('expert', 'dp')), may hold values 0 or 1
- hidden_act: bfloat16 [32, 288, 7168], P('expert', 'dp', 'tensor'), may hold values from -3 to 3
- down_weight: bfloat16 [32, 7168, 2048], P('expert', 'tensor', 'dp'), may hold values from -0.0625 to 0.0625
Outputs:
- grad_down: bfloat16 [32, 7168, 2048], P('expert', 'tensor', 'dp')
- grad_hidden: bfloat16 [32, 288, 7168], P('expert', 'dp', 'tensor')
- gate_grad: float32 [4096, 2], P(('expert', 'dp'))
The draws below stay inside these ranges and needn't reach their ends.
Inputs may be any that keep to these rules, and one draw needn't show every extreme that they name: `expert_ids`: each row names two different experts; among the 512 rows of one device no expert is named more than 36 times, and in every draw some device names some expert exactly 36 times.
All inputs are finite; a program needn't handle non-finite values. No bound on the sum of `keep` on one device may be relied on, other than what follows from the above.
Results may differ from the reference program's by a relative error of at most 0.0064.
Values may be sent and summed in bfloat16 or wider, within the bound.
A program may use at most 256 MiB of HBM per device.

```python
import math
import jax
import jax.numpy as jnp
import numpy as np
from jax import lax

D = 2048
FF = 7168
EXPERTS = 32
TOK_DEV = 512
CAP = 36
SLOTS = 144
TOKENS = 4096
N_EXPERT = 4
N_DP = 2


def place_ends(entries, stream_key, low, high):
    longest = entries.shape.index(max(entries.shape))
    spots = []
    for shift in (0, 1):
        where = [jax.random.randint(jax.random.fold_in(stream_key, axis), (), 0, length) for axis, length in enumerate(entries.shape)]
        where[longest] = (where[longest] + shift) % entries.shape[longest]
        spots.append(tuple(where))
    return entries.at[spots[0]].set(low).at[spots[1]].set(high)


def block_levels(rng, dims, shards, smallest, largest):
    gain, own = 1.0, jax.random.fold_in(rng, 6)
    for dim, parts in shards:
        draws = jnp.exp(jax.random.uniform(jax.random.fold_in(own, dim), (parts,), jnp.float32, smallest / len(shards), largest / len(shards)))
        gain = gain * jnp.repeat(draws, dims[dim] // parts).reshape([-1 if axis == dim else 1 for axis in range(len(dims))])
    return gain


def routed_block(own_key, own, number, rows, count, top, most, slope):
    order = jax.random.permutation(own_key, count)
    crowded, common = portions_of(count, rows * top, most, slope, True), portions_of(count, rows * top, most, slope, False)
    places = jnp.arange(count)

    def named(sizes, offset_by):
        used = int((sizes > 0).sum())
        fixed = max(1, used // 4)
        moved = fixed + (places - fixed + offset_by * (used - fixed)) % max(1, count - fixed)
        return jnp.zeros((count,), jnp.int32).at[order[jnp.where(places < fixed, places, moved)]].set(jnp.asarray(sizes, jnp.int32))

    sizes = jnp.where(number % 4 == 0, named(crowded, number // 4), named(common, number - number // 4 - 1))
    mixed = jax.random.permutation(jax.random.fold_in(own, 3), count)
    source_of, taker = mixed[0:count // 2 * 2:2], mixed[1:count // 2 * 2:2]
    room = jnp.minimum(sizes[source_of] - 1, most - sizes[taker]) // 2
    room = jnp.where((source_of == order[0]) | (taker == order[0]) | (sizes[taker] == 0), 0, jnp.maximum(room, 0))
    moved = jax.random.randint(jax.random.fold_in(own, 4), (count // 2,), 0, 1 << 20) % (room + 1)
    sizes = sizes.at[source_of].add(-moved).at[taker].add(moved)
    members = jnp.searchsorted(jnp.cumsum(sizes), jnp.arange(rows * top), side="right").astype(jnp.int32)
    listing = members.reshape(top, rows).T
    listing = listing[jax.random.permutation(jax.random.fold_in(own, 1), rows)]
    offset_by = jax.random.randint(jax.random.fold_in(own, 2), (rows, 1), 0, top)
    return jnp.take_along_axis(listing, (jnp.arange(top)[None, :] + offset_by) % top, axis=1)


def portions_of(number_of, total, bound, slope, full):
    portions = [(1 << 20) // math.isqrt(rank ** slope) + 1 for rank in range(1, number_of + 1)]
    largest = bound if full else min(bound, max(-(-total // number_of), total * portions[0] // sum(portions)))
    least = 1 if total - largest >= number_of - 1 else 0
    holding, rest = [largest] + [least] * (number_of - 1), total - largest - least * (number_of - 1)
    while rest > 0:
        candidates = [i for i in range(1, number_of) if holding[i] < largest] or [i for i in range(1, number_of) if holding[i] < bound]
        pool, remaining = sum([portions[i] for i in candidates]), rest
        for i in candidates:
            extra = min(bound - holding[i], max(1, remaining * portions[i] // pool), rest)
            holding[i] = holding[i] + extra
            rest = rest - extra
    return np.array(holding)


def centred(rng, shape, width, bound, pieces=(), kind=jnp.bfloat16):
    loudness = block_levels(rng, shape, pieces, -0.22, 0.18) if pieces else 1.0
    entries = jax.random.normal(rng, shape, jnp.float32) * width * loudness
    return jnp.minimum(jnp.maximum(entries, -bound), bound).astype(kind)


def setup_inputs(seed: int = 0) -> dict:
    arg_keys = jax.random.split(jax.random.key(seed), 7)
    out_grad = centred(arg_keys[0], (TOKENS, D), 0.25, 1.5, ((0, 8), (1, 4)))
    expert_ids_keys = jax.random.split(jax.random.fold_in(arg_keys[1], 1), TOKENS // TOK_DEV)
    expert_ids_turns = jax.random.permutation(jax.random.fold_in(arg_keys[1], 3), TOKENS // TOK_DEV)
    expert_ids = jax.vmap(lambda own, number: routed_block(jax.random.fold_in(arg_keys[1], 2), own, number, TOK_DEV, EXPERTS, 2, CAP, 2))(expert_ids_keys, expert_ids_turns).reshape((TOKENS, 2))
    gate_weights = jnp.clip(jnp.exp(math.log(1.0) - 2.9957323 * jax.random.uniform(arg_keys[2], (TOKENS, 2), jnp.float32) ** block_levels(arg_keys[2], (TOKENS, 2), ((0, 8),), -0.2, 0.2)), 0.05, 1.0)
    keep = place_ends((jax.random.randint(arg_keys[3], (TOKENS, 2), 0, 8) < 7).astype(jnp.int32), jax.random.fold_in(arg_keys[3], 1), 0, 1)
    hidden_act = centred(arg_keys[4], (EXPERTS, N_DP * SLOTS, FF), 0.5, 3.0, ((0, 4), (1, 2), (2, 4)))
    down_weight = centred(arg_keys[5], (EXPERTS, FF, D), FF ** -0.5, 0.0625, ((0, 4), (1, 4), (2, 2)))
    return {"out_grad": out_grad, "expert_ids": expert_ids, "gate_weights": gate_weights, "keep": keep, "hidden_act": hidden_act, "down_weight": down_weight}


def reference(out_grad, expert_ids, gate_weights, keep, hidden_act, down_weight):
    blocks = N_EXPERT * N_DP
    chosen = expert_ids.reshape(blocks, TOK_DEV * 2)
    onehot = (chosen[:, :, None] == jnp.arange(EXPERTS, dtype=jnp.int32)[None, None, :]).astype(jnp.int32)
    ranking = jnp.cumsum(onehot, axis=1) - onehot
    slot_in = jnp.sum(ranking * onehot, axis=2).astype(jnp.int32)
    block_id = jnp.arange(blocks, dtype=jnp.int32)[:, None]
    source = block_id // N_DP
    replica = block_id % N_DP
    dest_row = (replica * SLOTS + source * CAP + slot_in).reshape(-1).astype(jnp.int32)
    dest_expert = chosen.reshape(-1).astype(jnp.int32)
    repeated = jnp.repeat(out_grad, 2, axis=0)
    routed = jnp.zeros((EXPERTS, N_DP * SLOTS, D), jnp.bfloat16).at[dest_expert, dest_row].set(repeated)
    kept_mask = keep.reshape(-1).astype(jnp.float32)
    scale_flat = (gate_weights.reshape(-1) * kept_mask).astype(jnp.bfloat16)
    slot_scale = jnp.zeros((EXPERTS, N_DP * SLOTS), jnp.bfloat16).at[dest_expert, dest_row].set(scale_flat)

    def per_expert(expert_index):
        slot_rows = routed[expert_index]
        slot_weight = slot_scale[expert_index].astype(jnp.float32)
        hidden_rows = hidden_act[expert_index]
        weight_matrix = down_weight[expert_index]
        backprop = jnp.dot(slot_rows, weight_matrix.T, preferred_element_type=jnp.float32)
        grad_rows = (slot_weight[:, None] * backprop).astype(jnp.bfloat16)
        scores = jnp.sum(backprop * hidden_rows.astype(jnp.float32), axis=1)
        scaled = (slot_weight[:, None] * slot_rows.astype(jnp.float32)).astype(jnp.bfloat16)
        summed = jnp.zeros((FF, D), jnp.float32)
        for replica_idx in range(N_DP):
            first_row = replica_idx * SLOTS
            dp_term = jnp.dot(hidden_rows[first_row:first_row + SLOTS].T, scaled[first_row:first_row + SLOTS], preferred_element_type=jnp.float32).astype(jnp.bfloat16)
            dp_term = lax.optimization_barrier(dp_term)
            summed = summed + dp_term.astype(jnp.float32)
        return grad_rows, summed.astype(jnp.bfloat16), scores

    grad_hidden, grad_down, scores = lax.map(per_expert, jnp.arange(EXPERTS, dtype=jnp.int32))
    gate_grad = (scores[dest_expert, dest_row] * kept_mask).reshape(TOKENS, 2)
    return grad_down, grad_hidden, gate_grad
```

```python
import functools

import jax
import jax.numpy as jnp
from jax import lax
from jax.experimental import pallas as pl
from jax.experimental.pallas import tpu as pltpu
from jax.sharding import PartitionSpec as P

CHUNKS = 1
VMEM_LIMIT = 56 * 1024 * 1024


def swap(value):
    return lax.ppermute(value, "dp", [(0, 1), (1, 0)])


def gather_rows(own_refs, peer_refs, rows, shards):
    slots = own_refs[0].shape[1]
    chunks = len(own_refs)
    part = own_refs[0].shape[2] // shards
    for c in range(chunks):
        for s in range(shards):
            to = pl.ds((s * chunks + c) * part, part)
            at = pl.ds(s * part, part)
            rows[pl.ds(0, slots), to] = own_refs[c][0, :, at]
            rows[pl.ds(slots, slots), to] = peer_refs[c][0, :, at]


def backprop_kernel(chunks, shards, *refs):
    own, peer = refs[:chunks], refs[chunks : 2 * chunks]
    own_w, peer_w, own_h, peer_h, weight, own_out, peer_out, score, rows = refs[2 * chunks :]
    slots = own_h.shape[1]
    gather_rows(own, peer, rows, shards)
    back = lax.dot_general(
        rows[...], weight[0], (((1,), (1,)), ((), ())), preferred_element_type=jnp.float32
    )
    mine, theirs = back[:slots], back[slots:]
    own_out[0] = (own_w[0] * mine).astype(jnp.bfloat16)
    peer_out[0] = (peer_w[0] * theirs).astype(jnp.bfloat16)
    score[0, pl.ds(0, slots), :] = jnp.sum(
        mine * own_h[0].astype(jnp.float32), axis=1, keepdims=True
    )
    score[0, pl.ds(slots, slots), :] = jnp.sum(
        theirs * peer_h[0].astype(jnp.float32), axis=1, keepdims=True
    )


def grad_kernel(chunks, shards, *refs):
    own, peer = refs[:chunks], refs[chunks : 2 * chunks]
    own_w, peer_w, own_h, peer_h, out, rows, hidden = refs[2 * chunks :]
    slots = own_h.shape[1]
    gather_rows(own, peer, rows, shards)
    for first, weight, source in ((0, own_w, own_h), (slots, peer_w, peer_h)):
        at = pl.ds(first, slots)
        rows[at, :] = (weight[0] * rows[at, :].astype(jnp.float32)).astype(jnp.bfloat16)
        hidden[at, :] = source[0]
    out[0] = lax.dot_general(
        hidden[...], rows[...], (((0,), (0,)), ((), ())), preferred_element_type=jnp.float32
    ).astype(jnp.bfloat16)


def per_expert(array):
    return pl.BlockSpec((1,) + array.shape[1:], lambda e: (e, 0, 0))


def call(kernel, inputs, outputs, scratch, flops):
    moved = sum(a.size * a.dtype.itemsize for a in (*inputs, *outputs))
    return pl.pallas_call(
        kernel,
        grid=(inputs[0].shape[0],),
        in_specs=[per_expert(a) for a in inputs],
        out_specs=[per_expert(a) for a in outputs],
        out_shape=outputs,
        scratch_shapes=scratch,
        compiler_params=pltpu.CompilerParams(vmem_limit_bytes=VMEM_LIMIT),
        cost_estimate=pl.CostEstimate(flops=flops, bytes_accessed=moved, transcendentals=0),
    )(*inputs)


def body(out_grad, expert_ids, gate_weights, keep, hidden_act, down_weight):
    token_count, shard = out_grad.shape
    experts = lax.axis_size("expert")
    tensor = lax.axis_size("tensor")
    local, slots, units = hidden_act.shape
    half = down_weight.shape[2]
    capacity = slots // experts
    total = experts * local * capacity
    dp_index = lax.axis_index("dp")
    peer_h = swap(hidden_act)

    chosen = expert_ids.reshape(-1)
    order = jnp.arange(chosen.shape[0], dtype=jnp.int32)
    earlier = (chosen[:, None] == chosen[None, :]) & (order[None, :] < order[:, None])
    slot = jnp.sum(earlier.astype(jnp.int32), axis=1)
    position = (chosen // local) * (capacity * local) + slot * local + chosen % local
    pair = position.reshape(token_count, 2)
    places = jnp.arange(total, dtype=jnp.int32)
    placing = (
        (places[:, None] == pair[:, 0][None, :]) | (places[:, None] == pair[:, 1][None, :])
    ).astype(jnp.bfloat16)
    kept_mask = keep.reshape(-1).astype(jnp.float32)
    scale_flat = (gate_weights.reshape(-1) * kept_mask).astype(jnp.bfloat16).astype(jnp.float32)
    hit = places[:, None] == position[None, :]
    slot_scale = jnp.sum(jnp.where(hit, scale_flat[None, :], 0.0), axis=1)
    own_w = lax.all_to_all(
        slot_scale.reshape(experts, capacity * local), "expert", 0, 0, tiled=True
    )
    own_w = own_w.reshape(slots, local).T[:, :, None]
    peer_w = swap(own_w.reshape(local, slots)).reshape(local, slots, 1)

    own, peer = [], []
    part = shard // CHUNKS
    for c in range(CHUNKS):
        gathered = lax.all_gather(
            out_grad[:, c * part : (c + 1) * part], "tensor", axis=1, tiled=True
        )
        outgoing = jnp.dot(placing, gathered, preferred_element_type=jnp.float32).astype(
            jnp.bfloat16
        )
        width = gathered.shape[1] // 2
        arrived = lax.all_to_all(
            outgoing.reshape(experts, capacity * local, 2 * width), "expert", 0, 0, tiled=True
        ).reshape(slots, local, 2 * width)
        theirs = lax.dynamic_slice_in_dim(arrived, (1 - dp_index) * width, width, 2)
        peer.append(swap(theirs.transpose(1, 0, 2)))
        mine = lax.dynamic_slice_in_dim(arrived, dp_index * width, width, 2)
        own.append(mine.transpose(1, 0, 2))

    sent = jax.ShapeDtypeStruct((local, slots, units), jnp.bfloat16)
    flops = 4 * local * slots * units * half
    rows = pltpu.VMEM((2 * slots, half), jnp.bfloat16)
    own_part, peer_part, partial = call(
        functools.partial(backprop_kernel, CHUNKS, tensor // 2),
        [*own, *peer, own_w, peer_w, hidden_act, peer_h, down_weight],
        [sent, sent, jax.ShapeDtypeStruct((local, 2 * slots, 1), jnp.float32)],
        [rows],
        flops,
    )
    come = swap(peer_part)

    every = lax.all_gather(partial.reshape(local, 2, slots), ("expert", "tensor", "dp"), axis=0)
    every = every.reshape(experts, tensor, 2, local, 2, experts, capacity)
    mine = lax.dynamic_index_in_dim(every, lax.axis_index("expert"), 5, keepdims=False)
    direct = lax.dynamic_index_in_dim(mine, dp_index, 2, keepdims=False)[:, :, :, 0]
    across = lax.dynamic_index_in_dim(mine, 1 - dp_index, 2, keepdims=False)[:, :, :, 1]
    scores = jnp.sum(direct + across, axis=1).transpose(0, 2, 1).reshape(-1)
    picked = jnp.sum(jnp.where(hit, scores[:, None], 0.0), axis=0)
    gate_grad = (picked * kept_mask).reshape(token_count, 2)

    (grad_down,) = call(
        functools.partial(grad_kernel, CHUNKS, tensor // 2),
        [*own, *peer, own_w, peer_w, hidden_act, peer_h],
        [jax.ShapeDtypeStruct(down_weight.shape, jnp.bfloat16)],
        [rows, pltpu.VMEM((2 * slots, units), jnp.bfloat16)],
        flops,
    )
    grad_hidden = (own_part.astype(jnp.float32) + come.astype(jnp.float32)).astype(jnp.bfloat16)
    return (grad_down, grad_hidden, gate_grad)


def solution(mesh):
    in_specs = (
        P(("expert", "dp"), "tensor"),
        P(("expert", "dp"), None),
        P(("expert", "dp"), None),
        P(("expert", "dp"), None),
        P("expert", "dp", "tensor"),
        P("expert", "tensor", "dp"),
    )
    out_specs = (
        P("expert", "tensor", "dp"),
        P("expert", "dp", "tensor"),
        P(("expert", "dp"), None),
    )
    return jax.shard_map(body, mesh=mesh, in_specs=in_specs, out_specs=out_specs, check_vma=False)
```

```python
import functools

import jax
import jax.numpy as jnp
from jax import lax
from jax.experimental import pallas as pl
from jax.experimental.pallas import tpu as pltpu
from jax.sharding import PartitionSpec as P

CHUNKS = 2
VMEM_LIMIT = 56 * 1024 * 1024


def swap(value):
    return lax.ppermute(value, "dp", [(0, 1), (1, 0)])


def gather_rows(own_refs, peer_refs, rows, shards):
    slots = own_refs[0].shape[1]
    chunks = len(own_refs)
    part = own_refs[0].shape[2] // shards
    for c in range(chunks):
        for s in range(shards):
            to = pl.ds((s * chunks + c) * part, part)
            at = pl.ds(s * part, part)
            rows[pl.ds(0, slots), to] = own_refs[c][0, :, at]
            rows[pl.ds(slots, slots), to] = peer_refs[c][0, :, at]


def backprop_kernel(chunks, shards, *refs):
    own, peer = refs[:chunks], refs[chunks : 2 * chunks]
    own_w, peer_w, own_h, peer_h, weight, own_out, peer_out, score, rows = refs[2 * chunks :]
    slots = own_h.shape[1]
    gather_rows(own, peer, rows, shards)
    back = lax.dot_general(
        rows[...], weight[0], (((1,), (1,)), ((), ())), preferred_element_type=jnp.float32
    )
    mine, theirs = back[:slots], back[slots:]
    own_out[0] = (own_w[0] * mine).astype(jnp.bfloat16)
    peer_out[0] = (peer_w[0] * theirs).astype(jnp.bfloat16)
    score[0, pl.ds(0, slots), :] = jnp.sum(
        mine * own_h[0].astype(jnp.float32), axis=1, keepdims=True
    )
    score[0, pl.ds(slots, slots), :] = jnp.sum(
        theirs * peer_h[0].astype(jnp.float32), axis=1, keepdims=True
    )


def grad_kernel(chunks, shards, *refs):
    own, peer = refs[:chunks], refs[chunks : 2 * chunks]
    own_w, peer_w, own_h, peer_h, out, rows, hidden = refs[2 * chunks :]
    slots = own_h.shape[1]
    gather_rows(own, peer, rows, shards)
    for first, weight, source in ((0, own_w, own_h), (slots, peer_w, peer_h)):
        at = pl.ds(first, slots)
        rows[at, :] = (weight[0] * rows[at, :].astype(jnp.float32)).astype(jnp.bfloat16)
        hidden[at, :] = source[0]
    out[0] = lax.dot_general(
        hidden[...], rows[...], (((0,), (0,)), ((), ())), preferred_element_type=jnp.float32
    ).astype(jnp.bfloat16)


def per_expert(array):
    return pl.BlockSpec((1,) + array.shape[1:], lambda e: (e, 0, 0))


def call(kernel, inputs, outputs, scratch, flops):
    moved = sum(a.size * a.dtype.itemsize for a in (*inputs, *outputs))
    return pl.pallas_call(
        kernel,
        grid=(inputs[0].shape[0],),
        in_specs=[per_expert(a) for a in inputs],
        out_specs=[per_expert(a) for a in outputs],
        out_shape=outputs,
        scratch_shapes=scratch,
        compiler_params=pltpu.CompilerParams(vmem_limit_bytes=VMEM_LIMIT),
        cost_estimate=pl.CostEstimate(flops=flops, bytes_accessed=moved, transcendentals=0),
    )(*inputs)


def body(out_grad, expert_ids, gate_weights, keep, hidden_act, down_weight):
    token_count, shard = out_grad.shape
    experts = lax.axis_size("expert")
    tensor = lax.axis_size("tensor")
    local, slots, units = hidden_act.shape
    half = down_weight.shape[2]
    capacity = slots // experts
    total = experts * local * capacity
    dp_index = lax.axis_index("dp")
    peer_h = swap(hidden_act)

    chosen = expert_ids.reshape(-1)
    order = jnp.arange(chosen.shape[0], dtype=jnp.int32)
    earlier = (chosen[:, None] == chosen[None, :]) & (order[None, :] < order[:, None])
    slot = jnp.sum(earlier.astype(jnp.int32), axis=1)
    position = (chosen // local) * (capacity * local) + slot * local + chosen % local
    pair = position.reshape(token_count, 2)
    places = jnp.arange(total, dtype=jnp.int32)
    placing = (
        (places[:, None] == pair[:, 0][None, :]) | (places[:, None] == pair[:, 1][None, :])
    ).astype(jnp.bfloat16)
    kept_mask = keep.reshape(-1).astype(jnp.float32)
    scale_flat = (gate_weights.reshape(-1) * kept_mask).astype(jnp.bfloat16).astype(jnp.float32)
    hit = places[:, None] == position[None, :]
    slot_scale = jnp.sum(jnp.where(hit, scale_flat[None, :], 0.0), axis=1)
    own_w = lax.all_to_all(
        slot_scale.reshape(experts, capacity * local), "expert", 0, 0, tiled=True
    )
    own_w = own_w.reshape(slots, local).T[:, :, None]
    peer_w = swap(own_w.reshape(local, slots)).reshape(local, slots, 1)

    own, peer = [], []
    part = shard // CHUNKS
    for c in range(CHUNKS):
        gathered = lax.all_gather(
            out_grad[:, c * part : (c + 1) * part], "tensor", axis=1, tiled=True
        )
        outgoing = jnp.dot(placing, gathered, preferred_element_type=jnp.float32).astype(
            jnp.bfloat16
        )
        width = gathered.shape[1] // 2
        arrived = lax.all_to_all(
            outgoing.reshape(experts, capacity * local, 2 * width), "expert", 0, 0, tiled=True
        ).reshape(slots, local, 2 * width)
        theirs = lax.dynamic_slice_in_dim(arrived, (1 - dp_index) * width, width, 2)
        peer.append(swap(theirs.transpose(1, 0, 2)))
        mine = lax.dynamic_slice_in_dim(arrived, dp_index * width, width, 2)
        own.append(mine.transpose(1, 0, 2))

    sent = jax.ShapeDtypeStruct((local, slots, units), jnp.bfloat16)
    flops = 4 * local * slots * units * half
    rows = pltpu.VMEM((2 * slots, half), jnp.bfloat16)
    own_part, peer_part, partial = call(
        functools.partial(backprop_kernel, CHUNKS, tensor // 2),
        [*own, *peer, own_w, peer_w, hidden_act, peer_h, down_weight],
        [sent, sent, jax.ShapeDtypeStruct((local, 2 * slots, 1), jnp.float32)],
        [rows],
        flops,
    )
    come = swap(peer_part)

    partial = partial.reshape(local, 2, slots)
    partial = lax.psum(jnp.where(dp_index == 0, partial, partial[:, ::-1]), ("tensor", "dp"))
    mine = lax.dynamic_index_in_dim(partial, dp_index, 1, keepdims=False)
    mine = mine.reshape(local, experts, capacity).transpose(1, 2, 0)
    scores = lax.all_to_all(
        mine.reshape(experts, capacity * local), "expert", 0, 0, tiled=True
    ).reshape(-1)
    picked = jnp.sum(jnp.where(hit, scores[:, None], 0.0), axis=0)
    gate_grad = (picked * kept_mask).reshape(token_count, 2)

    (grad_down,) = call(
        functools.partial(grad_kernel, CHUNKS, tensor // 2),
        [*own, *peer, own_w, peer_w, hidden_act, peer_h],
        [jax.ShapeDtypeStruct(down_weight.shape, jnp.bfloat16)],
        [rows, pltpu.VMEM((2 * slots, units), jnp.bfloat16)],
        flops,
    )
    grad_hidden = (own_part.astype(jnp.float32) + come.astype(jnp.float32)).astype(jnp.bfloat16)
    return (grad_down, grad_hidden, gate_grad)


def solution(mesh):
    in_specs = (
        P(("expert", "dp"), "tensor"),
        P(("expert", "dp"), None),
        P(("expert", "dp"), None),
        P(("expert", "dp"), None),
        P("expert", "dp", "tensor"),
        P("expert", "tensor", "dp"),
    )
    out_specs = (
        P("expert", "tensor", "dp"),
        P("expert", "dp", "tensor"),
        P(("expert", "dp"), None),
    )
    return jax.shard_map(body, mesh=mesh, in_specs=in_specs, out_specs=out_specs, check_vma=False)
```
